32 devices in a mesh: groups: 2 (over x), blk: 16 (over z, y, core).
Axes of the slice: x: 2, y: 2, z: 4, core: 2. Of those that a mesh axis runs over, the one named last changes fastest.
Arguments:
- walkers: bfloat16 [64, 65536], P(('groups', 'blk')), parts along dimension 0, may hold values from -6 to 6
- intersection_inv: bfloat16 [64, 4096], P(('groups', 'blk')), parts along dimension 0, may hold values from -0.75 to 0.75
- new_slot: int32 [64], P(('groups', 'blk')), parts along dimension 0, may hold values from 0 to 31, as said below
- cholesky: bfloat16 [2048, 64, 10240], P(('groups', 'blk')), parts along dimension 0, may hold values from -0.0234375 to 0.0234375
Outputs:
- moved_walkers: bfloat16 [64, 65536], P(('groups', 'blk')), parts along dimension 0
- moved_intersection_inv: bfloat16 [64, 4096], P(('groups', 'blk')), parts along dimension 0
- force_bias: float32 [64, 10240], P(('groups', 'blk')), parts along dimension 0
The draws below stay inside these ranges and needn't reach their ends.
There are 2 independent parts, one for each index of `groups`. The reference program is written for one: setup_inputs(seed, part) draws one part's arguments, and reference() takes and returns one part's arrays. A program takes and returns all parts, laid end to end along the dimension named above; each array names one. Nothing has to cross between parts.
Inputs may be any that keep to these rules, and one draw needn't show every extreme that they name: new_slot is a permutation; the new owner of walker w is new_slot[w] // 2; the 2 walkers of one device go to 2 different owners, and new_slot[w] % 2 == w % 2.
All inputs are finite; a program needn't handle non-finite values.
Results may differ from the reference program's by a relative error of at most 0.0028.
Values may be sent and summed in bfloat16 or wider, within the bound.
A program may use at most 128 MiB of HBM per device.

```python
import jax
import jax.numpy as jnp
from jax import lax

M = 1024
NOCC = 64
NCHOL = 10240
W_DEV = 2
W_TOTAL = 32
N_BLK = 16


def draw_new_slot(key, part):
    device_count = W_TOTAL // W_DEV
    key_one, key_two = jax.random.split(jax.random.fold_in(key, 17))
    rotation = jax.random.permutation(key_one, device_count)
    relabel = jax.random.permutation(key_two, device_count)
    device_ids = jnp.arange(W_TOTAL, dtype=jnp.int32) // W_DEV
    local_ids = jnp.arange(W_TOTAL, dtype=jnp.int32) % W_DEV
    owners = relabel[(rotation[device_ids] + local_ids) % device_count]
    return (owners * W_DEV + local_ids).astype(jnp.int32)


def steps_of(rng, dims, pieces, least, high):
    def one(position, parts):
        heights = jax.random.uniform(jax.random.fold_in(jax.random.fold_in(rng, 6), position), (parts,), jnp.float32, least / len(pieces), high / len(pieces))
        return jnp.repeat(jnp.exp(heights), dims[position] // parts).reshape((-1,) + (1,) * (len(dims) - position - 1))

    gain = one(*pieces[0])
    for cut in pieces[1:]:
        gain = gain * one(*cut)
    return gain


def noise(key, dims, scale, most, cuts=(), kind=jnp.bfloat16):
    drawn = jax.random.normal(key, dims, jnp.float32) * scale
    if len(cuts) > 0:
        drawn = steps_of(key, dims, cuts, -0.22, 0.18) * drawn
    return jnp.clip(drawn, min=-most, max=most).astype(kind)


def setup_inputs(seed: int = 0, part: int = 0) -> dict:
    keys = jax.random.split(jax.random.key(seed), 5)
    own_keys = jax.random.split(jax.random.fold_in(keys[4], part), 5)
    return {
        "walkers": noise(own_keys[0], (W_TOTAL, M * NOCC), 1.0, 6.0, ((0, 16),)),
        "intersection_inv": noise(own_keys[1], (W_TOTAL, NOCC * NOCC), NOCC ** -0.5, 0.75, ((0, 16),)),
        "new_slot": draw_new_slot(jax.random.fold_in(jax.random.fold_in(keys[4], part), 71), part),
        "cholesky": noise(own_keys[3], (M, NOCC, NCHOL), (M * NOCC) ** -0.5, 0.0234375, ((0, 16),)),
    }


def reference(walkers, intersection_inv, new_slot, cholesky):
    walker_total = walkers.shape[0]
    anchor = jnp.zeros((walker_total,), jnp.int32).at[new_slot].set(jnp.arange(walker_total, dtype=jnp.int32))
    moved_walkers = walkers[anchor]
    moved_inverse = intersection_inv[anchor]
    greens = jnp.einsum('wpj,wij->wpi', moved_walkers.reshape(walker_total, M, NOCC).astype(jnp.float32), moved_inverse.reshape(walker_total, NOCC, NOCC).astype(jnp.float32)).astype(jnp.bfloat16)
    blocks = greens.reshape(walker_total, N_BLK, (M // N_BLK) * NOCC).transpose(1, 0, 2)
    chol_blocks = cholesky.reshape(N_BLK, (M // N_BLK) * NOCC, NCHOL)

    def add_block(running, operands):
        return running + jnp.dot(operands[0], operands[1], preferred_element_type=jnp.float32), None

    force_bias, _ = lax.scan(add_block, jnp.zeros((walker_total, NCHOL), jnp.float32), (blocks, chol_blocks))
    return moved_walkers, moved_inverse, force_bias
```

```python
import functools

import jax
import jax.numpy as jnp
from jax import lax
from jax.experimental import pallas as pl
from jax.experimental.pallas import tpu as pltpu
from jax.sharding import PartitionSpec as P

MESH = pl.DeviceIdType.MESH
LANES = 128
MIB = 2**20


def kernel(
    n, wd, rows, tail, batches, per_batch, slots, anchor_rows,
    wk_ref, iv_ref, bd_ref, contrib_ref, chol_ref,
    moved_ref, force_ref,
    ring, gsend, grecv, wsend, wrecv, msend, arecv, anchor_v, anchor_s,
    gflat, green, ftmp, fsend, frecv,
    ring_sem, local_sem, send_sem, recv_sem,
):
    me = lax.axis_index("blk")
    wt = n * wd
    cols = ring.shape[2]
    tiles = cols // LANES
    span = tiles * per_batch
    chunks = batches * per_batch
    blk = wd * rows

    def fetch(c, k):
        return pltpu.make_async_copy(
            chol_ref.at[:, pl.ds(pl.multiple_of(c * cols, cols), cols)],
            ring.at[k],
            ring_sem.at[k],
        )

    def peers(body):
        def one(i, carry):
            body(lax.rem(me + i, n))
            return carry

        lax.fori_loop(1, n, one, 0)

    def push(src_of, dst, k):
        def one(to):
            pltpu.make_async_remote_copy(
                src_ref=src_of(to), dst_ref=dst,
                send_sem=send_sem.at[k], recv_sem=recv_sem.at[k],
                device_id={"blk": to}, device_id_type=MESH,
            ).start()

        peers(one)

    def drain(buf, sem):
        part = buf.at[pl.ds(0, n - 1)]
        pltpu.make_async_copy(part, part, sem).wait()

    barrier = pltpu.get_barrier_semaphore()
    peers(
        lambda to: pl.semaphore_signal(
            barrier, inc=1, device_id={"blk": to}, device_id_type=MESH
        )
    )

    for c in range(slots):
        fetch(c, c).start()

    group = min(n, 16)

    def make(g, carry):
        at = pl.multiple_of(g * group * rows, group * rows)
        for w in range(wd):
            x = lax.dot_general(
                wk_ref[w, pl.ds(at, group * rows), :], bd_ref[w],
                (((1,), (1,)), ((), ())), preferred_element_type=jnp.float32,
            ).astype(jnp.bfloat16)
            for d in range(group):
                gsend[g * group + d, w * rows:(w + 1) * rows, :] = x[d * rows:(d + 1) * rows]
        return carry

    lax.fori_loop(0, n // group, make, 0)

    pl.semaphore_wait(barrier, n - 1)
    push(lambda to: contrib_ref, arecv.at[me], 0)
    push(lambda to: gsend.at[to], grecv.at[me], 1)

    def lay(d, carry):
        at = pl.multiple_of(d * rows, rows)
        for w in range(wd):
            wsend[d, w * rows:(w + 1) * rows, :] = wk_ref[w, pl.ds(at, rows), :]
        wsend[d, blk:blk + tail, :] = iv_ref[d]
        return carry

    lax.fori_loop(0, n, lay, 0)
    arecv[me] = contrib_ref[...]
    grecv[me] = gsend[me]
    wrecv[me] = wsend[me]

    drain(arecv, recv_sem.at[0])

    def add(d, total):
        return total + arecv[d]

    anchor_v[...] = lax.fori_loop(0, n, add, jnp.zeros((anchor_rows, LANES), jnp.int32))
    to_scalar = pltpu.make_async_copy(anchor_v, anchor_s, local_sem)
    to_scalar.start()
    to_scalar.wait()

    drain(grecv, recv_sem.at[1])

    def source(s):
        return anchor_s[s // LANES, s % LANES] // wd

    def permute(d, carry):
        for w in range(wd):
            s = d * wd + w
            at = pl.multiple_of(s * rows, rows)
            gflat[pl.ds(at, rows), :] = grecv[
                source(s), w * rows:(w + 1) * rows, :
            ].astype(jnp.float32)
        return carry

    lax.fori_loop(0, n, permute, 0)
    for r in range(green.shape[1] // LANES):
        green[:, r * LANES:(r + 1) * LANES] = gflat[
            pl.ds(r, wt, stride=rows), :
        ].astype(jnp.bfloat16)

    def move(d, carry):
        for w in range(wd):
            msend[d, w * rows:(w + 1) * rows, :] = wrecv[
                source(d * wd + w), w * rows:(w + 1) * rows, :
            ]
        row = lax.broadcasted_iota(jnp.int32, (tail, LANES), 0)
        piece = jnp.zeros((tail, LANES), jnp.float32)
        for w in range(wd):
            got = wrecv[source(d * wd + w), blk:blk + tail, :].astype(jnp.float32)
            piece = jnp.where(row // (tail // wd) == w, got, piece)
        msend[d, blk:blk + tail, :] = piece.astype(jnp.bfloat16)
        return carry

    def step(c, carry):
        k = lax.rem(c, slots)
        b = c // per_batch
        q = lax.rem(c, per_batch)
        fetch(c, k).wait()
        acc = jnp.dot(green[...], ring[k], preferred_element_type=jnp.float32)

        @pl.when(c + slots < chunks)
        def _():
            fetch(c + slots, k).start()

        for j in range(tiles):
            ftmp[pl.ds(q * tiles + j, wt, stride=span), :] = acc[:, j * LANES:(j + 1) * LANES]

        @pl.when(c == 0)
        def _():
            push(lambda to: wsend.at[to], wrecv.at[me], 2)

        @pl.when(c == min(chunks - 1, 6))
        def _():
            drain(wrecv, recv_sem.at[2])
            lax.fori_loop(0, n, move, 0)
            push(lambda to: msend.at[to], moved_ref.at[me], 3)
            moved_ref[me] = msend[me]

        @pl.when(q == per_batch - 1)
        def _():
            size = wd * span

            def cast(d, carry):
                at = pl.multiple_of(d * size, size)
                fsend[b, d] = ftmp[pl.ds(at, size), :].astype(jnp.bfloat16)
                return carry

            lax.fori_loop(0, n, cast, 0)
            force_ref[b] = ftmp[pl.ds(pl.multiple_of(me * size, size), size), :]
            push(lambda to: fsend.at[b, to], frecv.at[b, me], 4 + b)

        return carry

    lax.fori_loop(0, chunks, step, 0)

    def finish(b, carry):
        drain(frecv.at[b], recv_sem.at[4 + b])

        def plus(i, total):
            return total + frecv[b, lax.rem(me + i, n)].astype(jnp.float32)

        force_ref[b] = lax.fori_loop(1, n, plus, force_ref[b])
        return carry

    lax.fori_loop(0, batches, finish, 0)
    drain(moved_ref, recv_sem.at[3])
    drain(arecv, send_sem.at[0])
    drain(gsend, send_sem.at[1])
    drain(wsend, send_sem.at[2])
    drain(msend, send_sem.at[3])

    def sent(b, carry):
        drain(fsend.at[b], send_sem.at[4 + b])
        return carry

    lax.fori_loop(0, batches, sent, 0)


def local(walkers, intersection_inv, new_slot, cholesky):
    n = lax.axis_size("blk")
    me = lax.axis_index("blk")
    wd = walkers.shape[0]
    wt = n * wd
    orbitals, occ, ncol = cholesky.shape
    depth = orbitals * occ
    real = depth // LANES
    rows = -(-real // 16) * 16
    chol = cholesky.reshape(depth, ncol)

    wk = walkers.reshape(wd, n * real, LANES)
    if rows != real:
        wk = jnp.pad(
            wk.reshape(wd, n, real, LANES), ((0, 0), (0, 0), (0, rows - real), (0, 0))
        ).reshape(wd, n * rows, LANES)
    inv = intersection_inv.reshape(wd, occ, occ)
    pack = LANES // occ
    eye = jnp.eye(pack, dtype=jnp.bfloat16)
    bd = (eye[None, :, None, :, None] * inv[:, None, :, None, :]).reshape(wd, LANES, LANES)
    share = occ * occ // n
    part = max(16 // wd, -(-share // LANES))
    tail = wd * part
    iv = jnp.pad(
        intersection_inv.reshape(wd, n, share).transpose(1, 0, 2),
        ((0, 0), (0, 0), (0, part * LANES - share)),
    ).reshape(n, tail, LANES)
    anchor_rows = 8 * -(-wt // (8 * LANES))
    place = lax.broadcasted_iota(jnp.int32, (anchor_rows, LANES), 0) * LANES
    place = place + lax.broadcasted_iota(jnp.int32, (anchor_rows, LANES), 1)
    contrib = jnp.zeros((anchor_rows, LANES), jnp.int32)
    for w in range(wd):
        contrib = jnp.where(place == new_slot[w], me * wd + w, contrib)

    cols = 512
    per_batch = 4 if ncol % 2048 == 0 else 2
    chunks = ncol // cols
    batches = chunks // per_batch
    span = per_batch * cols // LANES
    bf, f32 = jnp.bfloat16, jnp.float32
    blk = wd * rows
    bufs = [
        ((n, blk, LANES), bf),
        ((n, blk, LANES), bf),
        ((n, blk + tail, LANES), bf),
        ((n, blk + tail, LANES), bf),
        ((n, blk + tail, LANES), bf),
        ((n, anchor_rows, LANES), jnp.int32),
        ((anchor_rows, LANES), jnp.int32),
    ]
    more = [
        ((wt * rows, LANES), f32),
        ((wt, depth), bf),
        ((wt * span, LANES), f32),
        ((batches, n, wd * span, LANES), bf),
        ((batches, n, wd * span, LANES), bf),
    ]

    def size(shape, dtype):
        total = jnp.dtype(dtype).itemsize
        for d in shape:
            total *= d
        return total

    used = sum(size(*b) for b in bufs + more)
    used += 2 * size((n, blk + tail, LANES), bf) + size((wd, ncol), f32)
    slots = min(chunks, (56 * MIB - used) // size((depth, cols), bf))

    vmem = pl.BlockSpec(memory_space=pltpu.VMEM)
    moved, force = pl.pallas_call(
        functools.partial(
            kernel, n, wd, rows, tail, batches, per_batch, slots, anchor_rows
        ),
        out_shape=(
            jax.ShapeDtypeStruct((n, blk + tail, LANES), bf),
            jax.ShapeDtypeStruct((batches, wd * span, LANES), f32),
        ),
        in_specs=[vmem, vmem, vmem, vmem, pl.BlockSpec(memory_space=pl.ANY)],
        out_specs=(vmem, vmem),
        scratch_shapes=[
            pltpu.VMEM((slots, depth, cols), bf),
            *[pltpu.VMEM(*b) for b in bufs],
            pltpu.SMEM((anchor_rows, LANES), jnp.int32),
            *[pltpu.VMEM(*b) for b in more],
            pltpu.SemaphoreType.DMA((slots,)),
            pltpu.SemaphoreType.DMA,
            pltpu.SemaphoreType.DMA((4 + batches,)),
            pltpu.SemaphoreType.DMA((4 + batches,)),
        ],
        compiler_params=pltpu.CompilerParams(
            collective_id=0, has_side_effects=True, vmem_limit_bytes=60 * MIB
        ),
        cost_estimate=pl.CostEstimate(
            flops=2 * wt * depth * ncol, bytes_accessed=2 * depth * ncol, transcendentals=0
        ),
    )(wk, iv, bd, contrib, chol)

    moved_walk = (
        moved[:, :blk].reshape(n, wd, rows, LANES)[:, :, :real]
        .transpose(1, 0, 2, 3).reshape(wd, n * depth)
    )
    moved_inverse = (
        moved[:, blk:].reshape(n, wd, part * LANES)[:, :, :share]
        .transpose(1, 0, 2).reshape(wd, occ * occ)
    )
    force_bias = (
        force.reshape(batches, wd, span * LANES).transpose(1, 0, 2).reshape(wd, ncol)
    )
    return (moved_walk, moved_inverse, force_bias)


def solution(mesh):
    placed = (
        P(("groups", "blk"), None),
        P(("groups", "blk"), None),
        P(("groups", "blk")),
        P(("groups", "blk"), None, None),
    )
    return jax.shard_map(
        local,
        mesh=mesh,
        in_specs=placed,
        out_specs=(
            P(("groups", "blk"), None),
            P(("groups", "blk"), None),
            P(("groups", "blk"), None),
        ),
        check_vma=False,
    )
```

```python
import functools

import jax
import jax.numpy as jnp
from jax import lax
from jax.experimental import pallas as pl
from jax.experimental.pallas import tpu as pltpu
from jax.sharding import PartitionSpec as P

MESH = pl.DeviceIdType.MESH
LANES = 128
MIB = 2**20


def kernel(
    n, wd, occ, rows, tail, batches, per_batch, slots, anchor_rows,
    wk_ref, iv_ref, slot_ref, chol_ref,
    walk_ref, piece_ref, force_ref,
    ring, gsend, grecv, wsend, wrecv, msend, mrecv, contrib, arecv, anchor_v,
    anchor_s, ivf, bdf, gflat, green, ftmp, xrecv, fsend, frecv, own,
    ring_sem, local_sem, send_sem, recv_sem,
):
    me = lax.axis_index("blk")
    wt = n * wd
    cols = ring.shape[2]
    tiles = cols // LANES
    span = tiles * per_batch
    chunks = batches * per_batch
    blk = wd * rows
    chips = n // 2
    chip, core = me // 2, lax.rem(me, 2)
    size = wd * span
    half = chips * size

    def fetch(c, k):
        return pltpu.make_async_copy(
            chol_ref.at[:, pl.ds(pl.multiple_of(c * cols, cols), cols)],
            ring.at[k],
            ring_sem.at[k],
        )

    def peers(body):
        def one(i, carry):
            body(lax.rem(me + i, n))
            return carry

        lax.fori_loop(1, n, one, 0)

    def push(src_of, dst, k):
        def one(to):
            pltpu.make_async_remote_copy(
                src_ref=src_of(to), dst_ref=dst,
                send_sem=send_sem.at[k], recv_sem=recv_sem.at[k],
                device_id={"blk": to}, device_id_type=MESH,
            ).start()

        peers(one)

    def drain(buf, sem, count):
        part = buf.at[pl.ds(0, count - 1)]
        pltpu.make_async_copy(part, part, sem).wait()

    barrier = pltpu.get_barrier_semaphore()
    peers(
        lambda to: pl.semaphore_signal(
            barrier, inc=1, device_id={"blk": to}, device_id_type=MESH
        )
    )

    for c in range(slots):
        fetch(c, c).start()

    place = lax.broadcasted_iota(jnp.int32, (anchor_rows, LANES), 0) * LANES
    place = place + lax.broadcasted_iota(jnp.int32, (anchor_rows, LANES), 1)
    mine = jnp.zeros((anchor_rows, LANES), jnp.int32)
    for w in range(wd):
        mine = jnp.where(place == slot_ref[w], me * wd + w, mine)
    contrib[...] = mine

    pack = LANES // occ
    deep = occ // pack
    flat = iv_ref[...].astype(jnp.float32)
    for t in range(deep):
        ivf[pl.ds(t, wd, stride=deep), :] = flat[:, t * LANES:(t + 1) * LANES]
    lane = lax.broadcasted_iota(jnp.int32, (deep, LANES), 1)
    for w in range(wd):
        v = ivf[w * deep:(w + 1) * deep, :]
        for e in range(pack):
            kept = jnp.where(lane // occ == e, v, 0.0)
            for h in range(pack):
                turned = kept if h == e else pltpu.roll(kept, (h - e) * occ % LANES, 1)
                bdf[pl.ds(w * LANES + h * occ + e, deep, stride=pack), :] = turned

    group = min(n, 16)
    bd = [bdf[w * LANES:(w + 1) * LANES, :].astype(jnp.bfloat16) for w in range(wd)]

    def make(g, carry):
        at = pl.multiple_of(g * group * rows, group * rows)
        for w in range(wd):
            x = lax.dot_general(
                wk_ref[w, pl.ds(at, group * rows), :], bd[w],
                (((1,), (1,)), ((), ())), preferred_element_type=jnp.float32,
            ).astype(jnp.bfloat16)
            for d in range(group):
                gsend[g * group + d, w * rows:(w + 1) * rows, :] = x[d * rows:(d + 1) * rows]
        return carry

    lax.fori_loop(0, n // group, make, 0)

    pl.semaphore_wait(barrier, n - 1)
    push(lambda to: contrib, arecv.at[me], 0)
    push(lambda to: gsend.at[to], grecv.at[me], 1)

    def lay(d, carry):
        at = pl.multiple_of(d * rows, rows)
        for w in range(wd):
            wsend[d, w * rows:(w + 1) * rows, :] = wk_ref[w, pl.ds(at, rows), :]
        row = lax.broadcasted_iota(jnp.int32, (tail, LANES), 0)
        share = jnp.zeros((tail, LANES), jnp.float32)
        for w in range(wd):
            for p in range(max(1, deep // n)):
                line = ivf[pl.ds(w * deep + d * deep // n + p, 1), :]
                share = jnp.where(row == w * (tail // wd) + p, line, share)
        wsend[d, blk:blk + tail, :] = share.astype(jnp.bfloat16)
        return carry

    lax.fori_loop(0, n, lay, 0)
    arecv[me] = mine
    grecv[me] = gsend[me]
    wrecv[me] = wsend[me]

    drain(arecv, recv_sem.at[0], n)

    def add(d, total):
        return total + arecv[d]

    anchor_v[...] = lax.fori_loop(0, n, add, jnp.zeros((anchor_rows, LANES), jnp.int32))
    to_scalar = pltpu.make_async_copy(anchor_v, anchor_s, local_sem)
    to_scalar.start()
    to_scalar.wait()

    drain(grecv, recv_sem.at[1], n)

    def source(s):
        return jnp.clip(anchor_s[s // LANES, s % LANES] // wd, 0, n - 1)

    def permute(d, carry):
        for w in range(wd):
            s = d * wd + w
            at = (lax.rem(d, 2) * chips + d // 2) * wd + w
            at = pl.multiple_of(at * rows, rows)
            gflat[pl.ds(at, rows), :] = grecv[
                source(s), w * rows:(w + 1) * rows, :
            ].astype(jnp.float32)
        return carry

    lax.fori_loop(0, n, permute, 0)
    for r in range(green.shape[1] // LANES):
        green[:, r * LANES:(r + 1) * LANES] = gflat[
            pl.ds(r, wt, stride=rows), :
        ].astype(jnp.bfloat16)

    def move(d, carry):
        for w in range(wd):
            msend[d, w * rows:(w + 1) * rows, :] = wrecv[
                source(d * wd + w), w * rows:(w + 1) * rows, :
            ]
        row = lax.broadcasted_iota(jnp.int32, (tail, LANES), 0)
        piece = jnp.zeros((tail, LANES), jnp.float32)
        for w in range(wd):
            got = wrecv[source(d * wd + w), blk:blk + tail, :].astype(jnp.float32)
            piece = jnp.where(row // (tail // wd) == w, got, piece)
        msend[d, blk:blk + tail, :] = piece.astype(jnp.bfloat16)
        return carry

    def swap(b):
        at = pl.multiple_of((1 - core) * half, half)
        return pltpu.make_async_remote_copy(
            src_ref=ftmp.at[b, pl.ds(at, half)], dst_ref=xrecv.at[b],
            send_sem=send_sem.at[4 + batches + b], recv_sem=recv_sem.at[4 + batches + b],
            device_id={"blk": chip * 2 + 1 - core}, device_id_type=MESH,
        )

    def combine(b):
        swap(b).wait_recv()

        def pair(p):
            mine = pl.multiple_of(core * half + p * size, size)
            other = pl.multiple_of(p * size, size)
            return ftmp[b, pl.ds(mine, size), :] + xrecv[b, pl.ds(other, size), :]

        def cast(p, carry):
            fsend[b, p] = pair(p).astype(jnp.bfloat16)
            return carry

        lax.fori_loop(0, chips, cast, 0)
        own[b] = pair(chip)

        def one(i, carry):
            p = lax.rem(chip + i, chips)
            pltpu.make_async_remote_copy(
                src_ref=fsend.at[b, p], dst_ref=frecv.at[b, chip],
                send_sem=send_sem.at[4 + b], recv_sem=recv_sem.at[4 + b],
                device_id={"blk": p * 2 + core}, device_id_type=MESH,
            ).start()
            return carry

        lax.fori_loop(1, chips, one, 0)

    def step(c, carry):
        k = lax.rem(c, slots)
        b = c // per_batch
        q = lax.rem(c, per_batch)
        fetch(c, k).wait()
        acc = jnp.dot(green[...], ring[k], preferred_element_type=jnp.float32)

        @pl.when(c + slots < chunks)
        def _():
            fetch(c + slots, k).start()

        for j in range(tiles):
            ftmp[b, pl.ds(q * tiles + j, wt, stride=span), :] = acc[:, j * LANES:(j + 1) * LANES]

        @pl.when(c == 0)
        def _():
            push(lambda to: wsend.at[to], wrecv.at[me], 2)

        @pl.when(c == min(chunks - 1, 6))
        def _():
            drain(wrecv, recv_sem.at[2], n)
            lax.fori_loop(0, n, move, 0)
            push(lambda to: msend.at[to], mrecv.at[me], 3)
            mrecv[me] = msend[me]

        @pl.when((q == 1) & (b > 0))
        def _():
            combine(b - 1)

        @pl.when(q == per_batch - 1)
        def _():
            swap(b).start()

        return carry

    lax.fori_loop(0, chunks, step, 0)
    combine(batches - 1)

    drain(mrecv, recv_sem.at[3], n)

    def keep(d, carry):
        at = pl.multiple_of(d * rows, rows)
        for w in range(wd):
            walk_ref[w, pl.ds(at, rows), :] = mrecv[d, w * rows:(w + 1) * rows, :]
        piece_ref[d] = mrecv[d, blk:blk + tail, :]
        return carry

    lax.fori_loop(0, n, keep, 0)

    def finish(b, carry):
        drain(frecv.at[b], recv_sem.at[4 + b], chips)

        def plus(i, total):
            return total + frecv[b, lax.rem(chip + i, chips)].astype(jnp.float32)

        total = lax.fori_loop(1, chips, plus, own[b])
        at = pl.multiple_of(b * span, span)
        for w in range(wd):
            force_ref[w, pl.ds(at, span), :] = total[w * span:(w + 1) * span]
        return carry

    lax.fori_loop(0, batches, finish, 0)
    drain(arecv, send_sem.at[0], n)
    drain(gsend, send_sem.at[1], n)
    drain(wsend, send_sem.at[2], n)
    drain(msend, send_sem.at[3], n)

    def sent(b, carry):
        drain(fsend.at[b], send_sem.at[4 + b], chips)
        swap(b).wait_send()
        return carry

    lax.fori_loop(0, batches, sent, 0)


def local(walkers, intersection_inv, new_slot, cholesky):
    n = lax.axis_size("blk")
    wd = walkers.shape[0]
    wt = n * wd
    orbitals, occ, ncol = cholesky.shape
    depth = orbitals * occ
    real = depth // LANES
    rows = -(-real // 16) * 16
    chol = cholesky.reshape(depth, ncol)

    wk = walkers.reshape(wd, n * real, LANES)
    if rows != real:
        wk = jnp.pad(
            wk.reshape(wd, n, real, LANES), ((0, 0), (0, 0), (0, rows - real), (0, 0))
        ).reshape(wd, n * rows, LANES)
    deep = occ * occ // LANES
    part = max(16 // wd, -(-deep // n))
    tail = wd * part
    anchor_rows = 8 * -(-wt // (8 * LANES))

    cols = 512
    per_batch = 4 if ncol % 2048 == 0 else 2
    chunks = ncol // cols
    batches = chunks // per_batch
    span = per_batch * cols // LANES
    bf, f32 = jnp.bfloat16, jnp.float32
    blk = wd * rows
    bufs = [
        ((n, blk, LANES), bf),
        ((n, blk, LANES), bf),
        ((n, blk + tail, LANES), bf),
        ((n, blk + tail, LANES), bf),
        ((n, blk + tail, LANES), bf),
        ((n, blk + tail, LANES), bf),
        ((anchor_rows, LANES), jnp.int32),
        ((n, anchor_rows, LANES), jnp.int32),
        ((anchor_rows, LANES), jnp.int32),
    ]
    more = [
        ((wd * deep, LANES), f32),
        ((wd * LANES, LANES), f32),
        ((wt * rows, LANES), f32),
        ((wt, depth), bf),
        ((batches, wt * span, LANES), f32),
        ((batches, wt * span // 2, LANES), f32),
        ((batches, n // 2, wd * span, LANES), bf),
        ((batches, n // 2, wd * span, LANES), bf),
        ((batches, wd * span, LANES), f32),
    ]

    def size(shape, dtype):
        total = jnp.dtype(dtype).itemsize
        for d in shape:
            total *= d
        return total

    used = sum(size(*b) for b in bufs + more)
    used += 2 * size((n, blk + tail, LANES), bf) + size((wd, ncol), f32)
    slots = min(chunks, (56 * MIB - used) // size((depth, cols), bf))

    vmem = pl.BlockSpec(memory_space=pltpu.VMEM)
    walk, piece, force = pl.pallas_call(
        functools.partial(
            kernel, n, wd, occ, rows, tail, batches, per_batch, slots, anchor_rows
        ),
        out_shape=(
            jax.ShapeDtypeStruct((wd, n * rows, LANES), bf),
            jax.ShapeDtypeStruct((n, tail, LANES), bf),
            jax.ShapeDtypeStruct((wd, ncol // LANES, LANES), f32),
        ),
        in_specs=[
            vmem, vmem,
            pl.BlockSpec(memory_space=pltpu.SMEM),
            pl.BlockSpec(memory_space=pl.ANY),
        ],
        out_specs=(vmem, vmem, vmem),
        scratch_shapes=[
            pltpu.VMEM((slots, depth, cols), bf),
            *[pltpu.VMEM(*b) for b in bufs],
            pltpu.SMEM((anchor_rows, LANES), jnp.int32),
            *[pltpu.VMEM(*b) for b in more],
            pltpu.SemaphoreType.DMA((slots,)),
            pltpu.SemaphoreType.DMA,
            pltpu.SemaphoreType.DMA((4 + 2 * batches,)),
            pltpu.SemaphoreType.DMA((4 + 2 * batches,)),
        ],
        compiler_params=pltpu.CompilerParams(
            collective_id=0, has_side_effects=True, vmem_limit_bytes=60 * MIB
        ),
        cost_estimate=pl.CostEstimate(
            flops=2 * wt * depth * ncol, bytes_accessed=2 * depth * ncol, transcendentals=0
        ),
    )(wk, intersection_inv, new_slot, chol)

    if rows != real:
        walk = walk.reshape(wd, n, rows, LANES)[:, :, :real]
    moved_walk = walk.reshape(wd, n * depth)
    took = max(1, deep // n)
    moved_inverse = (
        piece.reshape(n, wd, part, LANES)[::max(1, n // deep), :, :took]
        .transpose(1, 0, 2, 3).reshape(wd, occ * occ)
    )
    force_bias = force.reshape(wd, ncol)
    return (moved_walk, moved_inverse, force_bias)


def solution(mesh):
    placed = (
        P(("groups", "blk"), None),
        P(("groups", "blk"), None),
        P(("groups", "blk")),
        P(("groups", "blk"), None, None),
    )
    return jax.shard_map(
        local,
        mesh=mesh,
        in_specs=placed,
        out_specs=(
            P(("groups", "blk"), None),
            P(("groups", "blk"), None),
            P(("groups", "blk"), None),
        ),
        check_vma=False,
    )
```
